32 devices in a mesh: group: 2 (over y), expert: 16 (over z, x, core).
Axes of the slice: x: 2, y: 2, z: 4, core: 2. Of those that a mesh axis runs over, the one named last changes fastest.
Arguments:
- inputs: bfloat16 [3, 256, 2048], P(None, ('group', 'expert')), may hold values from -6 to 6
- queries: bfloat16 [3, 256, 2048], P(None, ('group', 'expert')), may hold values from -24 to 24
- new_keys: bfloat16 [3, 256, 128], P(None, ('group', 'expert')), may hold values from -8 to 8
- new_values: bfloat16 [3, 256, 128], P(None, ('group', 'expert')), may hold values from -6 to 6
- key_cache: bfloat16 [256, 384, 128], P(('group', 'expert')), may hold values from -4.5 to 4.5
- value_cache: bfloat16 [256, 384, 128], P(('group', 'expert')), may hold values from -6 to 6
- cache_lengths: int32 [256], P(('group', 'expert')), may hold values from 48 to 384, as said below
- expert_ids: int32 [3, 256, 8], P(None, ('group', 'expert')), may hold values from 0 to 15, all different within a row; in each aligned block of 8 rows (0 to 7, 8 to 15, ..., all dimensions but the last counted through in order) at most 8 rows name the same one
- route_weights: float32 [3, 256, 8], P(None, ('group', 'expert')), may hold values from 0.03 to 0.5
- w_gate: bfloat16 [16, 2048, 768], P('expert', 'group'), may hold values from -0.125 to 0.125
- w_up: bfloat16 [16, 2048, 768], P('expert', 'group'), may hold values from -0.125 to 0.125
- w_down: bfloat16 [16, 768, 2048], P('expert', None, 'group'), may hold values from -0.21875 to 0.21875
Outputs:
- layer_out: bfloat16 [3, 256, 2048], P(None, ('group', 'expert'))
The draws below stay inside these ranges and needn't reach their ends.
Inputs may be any that keep to these rules, and one draw needn't show every extreme that they name: `expert_ids`: in each step, no expert is named by more than 8 of the 8 rows of one aligned block. `cache_lengths`: in each aligned block of 8 rows one row has all 384 positions valid.
All inputs are finite; a program needn't handle non-finite values.
Results may differ from the reference program's by a relative error of at most 0.014.
Values may be sent and summed in bfloat16 or wider, within the bound.
A program may use at most 64 MiB of HBM per device.

```python
import math
import jax
import jax.numpy as jnp
import numpy as np
from jax import lax

D = 2048
FF = 768
HEADS = 32
KV_HEADS = 2
HEAD_DIM = 64
TOPK = 8
CACHE = 384
STEPS = 3
ROWS_DEV = 8
EXPERTS = 16
ROWS = 256
CAP = 8


def drawn(key):
    base_key = jax.random.fold_in(key, 7)
    key_cache_draw, key_query = jax.random.split(base_key, 2)
    feature_dim = KV_HEADS * HEAD_DIM
    cache_vals = jnp.clip(jax.random.normal(key_cache_draw, (ROWS, CACHE, feature_dim), jnp.float32), -4.5, 4.5)
    query_vals = jnp.clip(jax.random.normal(key_query, (STEPS, ROWS, HEADS * HEAD_DIM), jnp.float32), -4.5, 4.5)
    return (cache_vals, query_vals)


def draw_key_cache(key, part):
    return drawn(key)[0].astype(jnp.bfloat16)


def draw_queries(key, part):
    return drawn(key)[1].astype(jnp.bfloat16)


def draw_cache_lengths(key, part):
    key_one, key_two = jax.random.split(jax.random.fold_in(key, 3))
    lengths = jax.random.randint(key_one, (ROWS,), CACHE // 8, CACHE + 1)
    full_row = jax.random.randint(key_two, (ROWS // ROWS_DEV,), 0, ROWS_DEV)
    inside = jnp.arange(ROWS) % ROWS_DEV
    return jnp.where(inside == jnp.repeat(full_row, ROWS_DEV), CACHE, lengths).astype(jnp.int32)


def block_levels(stream_key, dims, cuts, smallest, largest):
    factor_of = 1.0
    for dim, shards_of in cuts:
        draws = jax.random.uniform(jax.random.fold_in(jax.random.fold_in(stream_key, 6), dim), (shards_of,), jnp.float32, smallest / len(cuts), largest / len(cuts))
        factor_of = factor_of * jnp.repeat(jnp.exp(draws), dims[dim] // shards_of).reshape((-1,) + (1,) * (len(dims) - 1 - dim))
    return factor_of


def deal_out(key, own, number, rows, amount, top, reach, lean):
    ranking = jax.random.permutation(key, amount)
    heavy_load, common = load_shares(amount, rows * top, reach, lean, True), load_shares(amount, rows * top, reach, lean, False)
    places = jnp.arange(amount)

    def named(sizes, rotation):
        used = int((sizes > 0).sum())
        fixed = max(1, used // 4)
        passed = fixed + (places - fixed + rotation * (used - fixed)) % max(1, amount - fixed)
        return jnp.zeros((amount,), jnp.int32).at[ranking[jnp.where(places < fixed, places, passed)]].set(jnp.asarray(sizes, jnp.int32))

    sizes = jnp.where(number % 4 == 0, named(heavy_load, number // 4), named(common, number - number // 4 - 1))
    mixed = jax.random.permutation(jax.random.fold_in(own, 3), amount)
    giver, taker = mixed[0:amount // 2 * 2:2], mixed[1:amount // 2 * 2:2]
    margin = jnp.minimum(sizes[giver] - 1, reach - sizes[taker]) // 2
    margin = jnp.where((giver == ranking[0]) | (taker == ranking[0]) | (sizes[taker] == 0), 0, jnp.maximum(margin, 0))
    passed = jax.random.randint(jax.random.fold_in(own, 4), (amount // 2,), 0, 1 << 20) % (margin + 1)
    sizes = sizes.at[giver].add(-passed).at[taker].add(passed)
    items = jnp.searchsorted(jnp.cumsum(sizes), jnp.arange(rows * top), side="right").astype(jnp.int32)
    listing = items.reshape(top, rows).T
    listing = listing[jax.random.permutation(jax.random.fold_in(own, 1), rows)]
    rotation = jax.random.randint(jax.random.fold_in(own, 2), (rows, 1), 0, top)
    return jnp.take_along_axis(listing, (jnp.arange(top)[None, :] + rotation) % top, axis=1)


def load_shares(amount, total, bound, lean, full):
    loads = [(1 << 20) // math.isqrt(rank ** lean) + 1 for rank in range(1, amount + 1)]
    largest = bound if full else min(bound, max(-(-total // amount), total * loads[0] // sum(loads)))
    least = 1 if total - largest >= amount - 1 else 0
    holding, surplus = [largest] + [least] * (amount - 1), total - largest - least * (amount - 1)
    while surplus > 0:
        candidates = [i for i in range(1, amount) if holding[i] < largest] or [i for i in range(1, amount) if holding[i] < bound]
        mass, left = sum([loads[i] for i in candidates]), surplus
        for i in candidates:
            addition = min(bound - holding[i], max(1, left * loads[i] // mass), surplus)
            holding[i] = holding[i] + addition
            surplus = surplus - addition
    return np.array(holding)


def bell_draw(rng, dims, scale, bound, cuts=(), kind=jnp.bfloat16):
    array = scale * jax.random.normal(rng, dims, jnp.float32)
    if cuts:
        array = array * block_levels(rng, dims, cuts, -0.22, 0.18)
    return jnp.clip(array, -bound, bound).astype(kind)


def setup_inputs(seed: int = 0) -> dict:
    key_list = jax.random.split(jax.random.key(seed), 13)
    inputs = bell_draw(key_list[0], (STEPS, ROWS, D), 1.0, 6.0, ((1, 32),))
    queries = draw_queries(jax.random.fold_in(key_list[12], 71), 0)
    new_keys = bell_draw(key_list[2], (STEPS, ROWS, KV_HEADS * HEAD_DIM), 2.0, 8.0, ((1, 32),))
    new_values = bell_draw(key_list[3], (STEPS, ROWS, KV_HEADS * HEAD_DIM), 1.0, 6.0, ((1, 32),))
    key_cache = draw_key_cache(jax.random.fold_in(key_list[12], 71), 0)
    value_cache = bell_draw(key_list[5], (ROWS, CACHE, KV_HEADS * HEAD_DIM), 1.0, 6.0, ((0, 32),))
    cache_lengths = draw_cache_lengths(jax.random.fold_in(key_list[12], 71), 0)
    expert_ids_keys = jax.random.split(jax.random.fold_in(key_list[7], 1), STEPS * ROWS // ROWS_DEV)
    expert_ids_turns = jax.random.permutation(jax.random.fold_in(key_list[7], 3), STEPS * ROWS // ROWS_DEV)
    expert_ids = jax.vmap(lambda own, number: deal_out(jax.random.fold_in(key_list[7], 2), own, number, ROWS_DEV, EXPERTS, TOPK, CAP, 2))(expert_ids_keys, expert_ids_turns).reshape((STEPS, ROWS, TOPK))
    route_weights = jnp.clip(jnp.exp(math.log(0.5) - 2.8134107 * jax.random.uniform(key_list[8], (STEPS, ROWS, TOPK), jnp.float32) ** block_levels(key_list[8], (STEPS, ROWS, TOPK), ((1, 32),), -0.2, 0.2)), 0.03, 0.5)
    w_gate = bell_draw(key_list[9], (EXPERTS, D, FF), D ** -0.5, 0.125, ((0, 16), (1, 2)))
    w_up = bell_draw(key_list[10], (EXPERTS, D, FF), D ** -0.5, 0.125, ((0, 16), (1, 2)))
    w_down = bell_draw(key_list[11], (EXPERTS, FF, D), FF ** -0.5, 0.21875, ((0, 16), (2, 2)))
    return dict(inputs=inputs, queries=queries, new_keys=new_keys, new_values=new_values, key_cache=key_cache, value_cache=value_cache, cache_lengths=cache_lengths, expert_ids=expert_ids, route_weights=route_weights, w_gate=w_gate, w_up=w_up, w_down=w_down)


def attend_block(query_vals, key_rows, value_rows, valid_mask):
    scores = jnp.einsum("bkgd,bjkd->bkgj", query_vals, key_rows) * (HEAD_DIM ** -0.5)
    scores = jnp.where(valid_mask[:, None, None, :], scores, -1e30)
    highest = jnp.max(scores, axis=-1, keepdims=True)
    weights = jnp.exp(scores - highest)
    probs = (weights / jnp.sum(weights, axis=-1, keepdims=True)).astype(jnp.bfloat16)
    return jnp.einsum("bkgj,bjkd->bkgd", probs.astype(jnp.float32), value_rows)


def reference(inputs, queries, new_keys, new_values, key_cache, value_cache, cache_lengths, expert_ids, route_weights, w_gate, w_up, w_down):
    per_group = HEADS // KV_HEADS
    row_block = math.gcd(ROWS, 512)
    num_blocks = ROWS // row_block
    limit = CAP * (ROWS // ROWS_DEV)
    results = []
    for step_index in range(STEPS):
        fresh = step_index + 1

        def one_block(pieces):
            query_b, key_b, value_b, fresh_k, fresh_v, length_b = pieces
            key_rows = jnp.concatenate([key_b, fresh_k], axis=1).astype(jnp.float32).reshape(row_block, CACHE + fresh, KV_HEADS, HEAD_DIM)
            value_rows = jnp.concatenate([value_b, fresh_v], axis=1).astype(jnp.float32).reshape(row_block, CACHE + fresh, KV_HEADS, HEAD_DIM)
            cache_ok = jnp.arange(CACHE, dtype=jnp.int32)[None, :] < length_b[:, None]
            valid_mask = jnp.concatenate([cache_ok, jnp.ones((row_block, fresh), dtype=bool)], axis=1)
            query_vals = query_b.astype(jnp.float32).reshape(row_block, KV_HEADS, per_group, HEAD_DIM)
            return attend_block(query_vals, key_rows, value_rows, valid_mask).reshape(row_block, D)

        attended = lax.map(one_block, (
            queries[step_index].reshape(num_blocks, row_block, D),
            key_cache.reshape(num_blocks, row_block, CACHE, KV_HEADS * HEAD_DIM),
            value_cache.reshape(num_blocks, row_block, CACHE, KV_HEADS * HEAD_DIM),
            jnp.swapaxes(new_keys[:fresh], 0, 1).reshape(num_blocks, row_block, fresh, KV_HEADS * HEAD_DIM),
            jnp.swapaxes(new_values[:fresh], 0, 1).reshape(num_blocks, row_block, fresh, KV_HEADS * HEAD_DIM),
            cache_lengths.reshape(num_blocks, row_block))).reshape(ROWS, D)
        hidden = (inputs[step_index].astype(jnp.float32) + attended).astype(jnp.bfloat16)
        flat_ids = expert_ids[step_index].reshape(-1)
        flat_weights = route_weights[step_index].reshape(-1)

        def one_expert(running, expert):
            matches = flat_ids == expert
            picked_at = jnp.nonzero(matches, size=limit, fill_value=0)[0].astype(jnp.int32)
            is_used = jnp.arange(limit, dtype=jnp.int32) < jnp.sum(matches.astype(jnp.int32))
            row_index = (picked_at // TOPK).astype(jnp.int32)
            tokens = hidden[row_index].astype(jnp.float32)
            gate_val = jnp.dot(tokens, w_gate[expert].astype(jnp.float32), precision=lax.Precision.HIGHEST)
            up_val = jnp.dot(tokens, w_up[expert].astype(jnp.float32), precision=lax.Precision.HIGHEST)
            activated = (jax.nn.silu(gate_val) * up_val).astype(jnp.bfloat16)
            expert_out = jnp.dot(activated.astype(jnp.float32), w_down[expert].astype(jnp.float32), precision=lax.Precision.HIGHEST).astype(jnp.bfloat16)
            factor = jnp.where(is_used, flat_weights[picked_at], jnp.zeros((), jnp.float32))
            return running.at[row_index].add(factor[:, None] * expert_out.astype(jnp.float32)), None

        running, _ = lax.scan(one_expert, jnp.zeros((ROWS, D), jnp.float32), jnp.arange(EXPERTS, dtype=jnp.int32))
        results.append((hidden.astype(jnp.float32) + running).astype(jnp.bfloat16))
    return jnp.stack(results)
```

```python
import jax
import jax.numpy as jnp
from jax import lax
from jax.sharding import PartitionSpec as P

HEADS = 32
KV_HEADS = 2
HEAD_DIM = 64
TOPK = 8
CACHE = 384
STEPS = 3


def attend_rows(query_vals, key_rows, value_rows, cache_ok, fresh_keys, fresh_values):
    factor = HEAD_DIM ** (-0.5)
    old_scores = (
        jnp.einsum("bkgd,bjkd->bkgj", query_vals, key_rows, preferred_element_type=jnp.float32)
        * factor
    )
    old_scores = jnp.where(cache_ok[:, None, None, :], old_scores, -1e30)
    new_scores = (
        jnp.einsum("bkgd,bjkd->bkgj", query_vals, fresh_keys, preferred_element_type=jnp.float32)
        * factor
    )
    highest = jnp.maximum(
        jnp.max(old_scores, axis=-1, keepdims=True), jnp.max(new_scores, axis=-1, keepdims=True)
    )
    old_weights = jnp.exp(old_scores - highest)
    new_weights = jnp.exp(new_scores - highest)
    denom_sum = jnp.sum(old_weights, axis=-1, keepdims=True) + jnp.sum(
        new_weights, axis=-1, keepdims=True
    )
    old_probs = (old_weights / denom_sum).astype(jnp.bfloat16)
    new_probs = (new_weights / denom_sum).astype(jnp.bfloat16)
    attended = jnp.einsum(
        "bkgj,bjkd->bkgd", old_probs, value_rows, preferred_element_type=jnp.float32
    )
    return attended + jnp.einsum(
        "bkgj,bjkd->bkgd", new_probs, fresh_values, preferred_element_type=jnp.float32
    )


def shards(
    inputs,
    queries,
    new_keys,
    new_values,
    key_cache,
    value_cache,
    cache_lengths,
    expert_ids,
    route_weights,
    w_gate,
    w_up,
    w_down,
):
    experts_all = lax.axis_size("expert")
    rows_dev = inputs.shape[1]
    per_group = HEADS // KV_HEADS
    capacity = max(2, 2 * rows_dev * TOPK // experts_all)
    gate_full, up_full, down_full = (
        lax.all_gather(w_gate, "group", axis=1, tiled=True),
        lax.all_gather(w_up, "group", axis=1, tiled=True),
        lax.all_gather(w_down, "group", axis=2, tiled=True),
    )
    gate_mat = gate_full[0]
    up_mat = up_full[0]
    down_mat = down_full[0]
    key_rows = key_cache.reshape(rows_dev, CACHE, KV_HEADS, HEAD_DIM)
    value_rows = value_cache.reshape(rows_dev, CACHE, KV_HEADS, HEAD_DIM)
    cache_ok = jnp.arange(CACHE, dtype=jnp.int32)[None, :] < cache_lengths[:, None]
    slot_columns = jnp.arange(experts_all * capacity, dtype=jnp.int32)
    expert_range = jnp.arange(experts_all, dtype=jnp.int32)
    results = []
    for step_index in range(STEPS):
        fresh = step_index + 1
        fresh_keys = jnp.swapaxes(new_keys[:fresh], 0, 1).reshape(
            rows_dev, fresh, KV_HEADS, HEAD_DIM
        )
        fresh_values = jnp.swapaxes(new_values[:fresh], 0, 1).reshape(
            rows_dev, fresh, KV_HEADS, HEAD_DIM
        )
        query_vals = queries[step_index].reshape(rows_dev, KV_HEADS, per_group, HEAD_DIM)
        attended = attend_rows(query_vals, key_rows, value_rows, cache_ok, fresh_keys, fresh_values)
        hidden = (inputs[step_index].astype(jnp.float32) + attended.reshape(rows_dev, -1)).astype(
            jnp.bfloat16
        )
        chosen = expert_ids[step_index].reshape(-1)
        onehot = (chosen[:, None] == expert_range[None, :]).astype(jnp.int32)
        before = jnp.cumsum(onehot, axis=0) - onehot
        slot_rank = jnp.sum(before * onehot, axis=1)
        target = chosen * capacity + slot_rank
        placed = (target[:, None] == slot_columns[None, :]).reshape(rows_dev, TOPK, -1)
        spread = jnp.any(placed, axis=1).astype(jnp.bfloat16)
        outgoing = jnp.einsum(
            "rc,rd->cd", spread, hidden, preferred_element_type=jnp.float32
        ).astype(jnp.bfloat16)
        outgoing = outgoing.reshape(experts_all, capacity, -1)
        mixing = jnp.sum(jnp.where(placed, route_weights[step_index][:, :, None], 0.0), axis=1)
        arrived = lax.all_to_all(outgoing, "expert", split_axis=0, concat_axis=0, tiled=True)
        num_slots, item_count, feature_dim = arrived.shape
        tokens = arrived.reshape(num_slots * item_count, feature_dim)
        gate_val = jnp.dot(tokens, gate_mat, preferred_element_type=jnp.float32)
        up_val = jnp.dot(tokens, up_mat, preferred_element_type=jnp.float32)
        activated = (jax.nn.silu(gate_val) * up_val).astype(jnp.bfloat16)
        expert_out = jnp.dot(activated, down_mat, preferred_element_type=jnp.float32).astype(
            jnp.bfloat16
        )
        returned = lax.all_to_all(
            expert_out.reshape(num_slots, item_count, feature_dim),
            "expert",
            split_axis=0,
            concat_axis=0,
            tiled=True,
        )
        combined = jnp.dot(
            mixing,
            returned.reshape(experts_all * capacity, -1).astype(jnp.float32),
            precision=lax.Precision.HIGHEST,
        )
        results.append((hidden.astype(jnp.float32) + combined).astype(jnp.bfloat16))
    return jnp.stack(results)


def dense_shards(
    inputs,
    queries,
    new_keys,
    new_values,
    key_cache,
    value_cache,
    cache_lengths,
    expert_ids,
    route_weights,
    w_gate,
    w_up,
    w_down,
):
    groups = lax.axis_size("group")
    experts_all = lax.axis_size("expert")
    me = lax.axis_index("group")
    rows_dev = inputs.shape[1]
    width = inputs.shape[2]
    part = w_gate.shape[2] // groups
    depth = w_gate.shape[1]
    columns = w_down.shape[2]
    gate_full = jnp.zeros((width, part), w_gate.dtype)
    up_full = jnp.zeros((width, part), w_gate.dtype)
    down_full = jnp.zeros((part, width), w_gate.dtype)
    pairs = []
    for shift in range(groups):
        target = lax.rem(me + shift, groups)
        pieces = (
            lax.dynamic_slice_in_dim(w_gate[0], target * part, part, 1),
            lax.dynamic_slice_in_dim(w_up[0], target * part, part, 1),
            lax.dynamic_slice_in_dim(w_down[0], target * part, part, 0),
        )
        if shift:
            perm = [(i, (i + shift) % groups) for i in range(groups)]
            pieces = tuple(lax.ppermute(piece, "group", perm) for piece in pieces)
        pairs.append((lax.rem(me - shift + groups, groups), pieces))
    for source, (gate_piece, up_piece, down_piece) in pairs:
        gate_full = lax.dynamic_update_slice_in_dim(gate_full, gate_piece, source * depth, 0)
        up_full = lax.dynamic_update_slice_in_dim(up_full, up_piece, source * depth, 0)
        down_full = lax.dynamic_update_slice_in_dim(down_full, down_piece, source * columns, 1)
    hidden = attend_steps(
        inputs, queries, new_keys, new_values, key_cache, value_cache, cache_lengths
    )
    expert_range = jnp.arange(experts_all, dtype=jnp.int32)
    mixing = jnp.sum(
        jnp.where(
            expert_ids[..., None] == expert_range, route_weights[..., None], jnp.float32(0.0)
        ),
        axis=2,
    )
    mixing = mixing.reshape(STEPS * rows_dev, experts_all)
    flat = hidden.reshape(STEPS * rows_dev, width)
    tokens = lax.all_gather(flat, ("group", "expert"), axis=0, tiled=True)
    factors = lax.all_gather(mixing, ("group", "expert"), axis=0, tiled=True)
    factor = lax.dynamic_slice_in_dim(factors, lax.axis_index("expert"), 1, 1)
    gate_val = jnp.dot(tokens, gate_full, preferred_element_type=jnp.float32)
    up_val = jnp.dot(tokens, up_full, preferred_element_type=jnp.float32)
    activated = (jax.nn.silu(gate_val) * up_val).astype(jnp.bfloat16)
    expert_out = jnp.dot(activated, down_full, preferred_element_type=jnp.float32)
    weighted = (factor * expert_out).astype(jnp.bfloat16)
    combined = lax.psum_scatter(weighted, ("group", "expert"), scatter_dimension=0, tiled=True)
    out = flat.astype(jnp.float32) + combined.astype(jnp.float32)
    return out.astype(jnp.bfloat16).reshape(STEPS, rows_dev, width)


def attend_steps(inputs, queries, new_keys, new_values, key_cache, value_cache, cache_lengths):
    rows_dev = inputs.shape[1]
    per_group = HEADS // KV_HEADS
    key_rows = jnp.concatenate([key_cache, jnp.swapaxes(new_keys, 0, 1)], axis=1).reshape(
        rows_dev, CACHE + STEPS, KV_HEADS, HEAD_DIM
    )
    value_rows = jnp.concatenate([value_cache, jnp.swapaxes(new_values, 0, 1)], axis=1).reshape(
        rows_dev, CACHE + STEPS, KV_HEADS, HEAD_DIM
    )
    query_vals = queries.reshape(STEPS, rows_dev, KV_HEADS, per_group, HEAD_DIM)
    scores = jnp.einsum(
        "tbkgd,bjkd->bktgj", query_vals, key_rows, preferred_element_type=jnp.float32
    ) * (HEAD_DIM ** (-0.5))
    place = jnp.arange(CACHE + STEPS, dtype=jnp.int32)
    step = jnp.arange(STEPS, dtype=jnp.int32)
    ok_old = place[None, None, :] < cache_lengths[:, None, None]
    ok_new = (place[None, :] >= CACHE) & (place[None, :] - CACHE <= step[:, None])
    ok = ok_old & (place < CACHE) | ok_new[None]
    scores = jnp.where(ok[:, None, :, None, :], scores, -1e30)
    highest = jnp.max(scores, axis=-1, keepdims=True)
    weights = jnp.exp(scores - highest)
    probs = (weights / jnp.sum(weights, axis=-1, keepdims=True)).astype(jnp.bfloat16)
    attended = jnp.einsum(
        "bktgj,bjkd->tbkgd", probs, value_rows, preferred_element_type=jnp.float32
    )
    return (inputs.astype(jnp.float32) + attended.reshape(inputs.shape)).astype(jnp.bfloat16)


def pick_plan(*args):
    rows_dev = args[0].shape[1]
    capacity = max(2, 2 * rows_dev * TOPK // lax.axis_size("expert"))
    if capacity >= rows_dev:
        return dense_shards(*args)
    return shards(*args)


def solution(mesh):
    in_specs = (
        P(None, ("group", "expert"), None),
        P(None, ("group", "expert"), None),
        P(None, ("group", "expert"), None),
        P(None, ("group", "expert"), None),
        P(("group", "expert"), None, None),
        P(("group", "expert"), None, None),
        P(("group", "expert")),
        P(None, ("group", "expert"), None),
        P(None, ("group", "expert"), None),
        P("expert", "group", None),
        P("expert", "group", None),
        P("expert", None, "group"),
    )
    out_specs = P(None, ("group", "expert"), None)
    return jax.shard_map(pick_plan, mesh=mesh, in_specs=in_specs, out_specs=out_specs, check_vma=False)
```

```python
import jax
import jax.numpy as jnp
from jax import lax
from jax.sharding import PartitionSpec as P

HEADS = 32
KV_HEADS = 2
HEAD_DIM = 64
TOPK = 8
CACHE = 384
STEPS = 3


def attend_rows(query_vals, key_rows, value_rows, cache_ok, fresh_keys, fresh_values):
    factor = HEAD_DIM ** (-0.5)
    old_scores = (
        jnp.einsum("bkgd,bjkd->bkgj", query_vals, key_rows, preferred_element_type=jnp.float32)
        * factor
    )
    old_scores = jnp.where(cache_ok[:, None, None, :], old_scores, -1e30)
    new_scores = (
        jnp.einsum("bkgd,bjkd->bkgj", query_vals, fresh_keys, preferred_element_type=jnp.float32)
        * factor
    )
    highest = jnp.maximum(
        jnp.max(old_scores, axis=-1, keepdims=True), jnp.max(new_scores, axis=-1, keepdims=True)
    )
    old_weights = jnp.exp(old_scores - highest)
    new_weights = jnp.exp(new_scores - highest)
    denom_sum = jnp.sum(old_weights, axis=-1, keepdims=True) + jnp.sum(
        new_weights, axis=-1, keepdims=True
    )
    old_probs = (old_weights / denom_sum).astype(jnp.bfloat16)
    new_probs = (new_weights / denom_sum).astype(jnp.bfloat16)
    attended = jnp.einsum(
        "bkgj,bjkd->bkgd", old_probs, value_rows, preferred_element_type=jnp.float32
    )
    return attended + jnp.einsum(
        "bkgj,bjkd->bkgd", new_probs, fresh_values, preferred_element_type=jnp.float32
    )


def shards(
    inputs,
    queries,
    new_keys,
    new_values,
    key_cache,
    value_cache,
    cache_lengths,
    expert_ids,
    route_weights,
    w_gate,
    w_up,
    w_down,
):
    experts_all = lax.axis_size("expert")
    rows_dev = inputs.shape[1]
    per_group = HEADS // KV_HEADS
    capacity = max(2, 2 * rows_dev * TOPK // experts_all)
    gate_full, up_full, down_full = (
        lax.all_gather(w_gate, "group", axis=1, tiled=True),
        lax.all_gather(w_up, "group", axis=1, tiled=True),
        lax.all_gather(w_down, "group", axis=2, tiled=True),
    )
    gate_mat = gate_full[0]
    up_mat = up_full[0]
    down_mat = down_full[0]
    key_rows = key_cache.reshape(rows_dev, CACHE, KV_HEADS, HEAD_DIM)
    value_rows = value_cache.reshape(rows_dev, CACHE, KV_HEADS, HEAD_DIM)
    cache_ok = jnp.arange(CACHE, dtype=jnp.int32)[None, :] < cache_lengths[:, None]
    slot_columns = jnp.arange(experts_all * capacity, dtype=jnp.int32)
    expert_range = jnp.arange(experts_all, dtype=jnp.int32)
    results = []
    for step_index in range(STEPS):
        fresh = step_index + 1
        fresh_keys = jnp.swapaxes(new_keys[:fresh], 0, 1).reshape(
            rows_dev, fresh, KV_HEADS, HEAD_DIM
        )
        fresh_values = jnp.swapaxes(new_values[:fresh], 0, 1).reshape(
            rows_dev, fresh, KV_HEADS, HEAD_DIM
        )
        query_vals = queries[step_index].reshape(rows_dev, KV_HEADS, per_group, HEAD_DIM)
        attended = attend_rows(query_vals, key_rows, value_rows, cache_ok, fresh_keys, fresh_values)
        hidden = (inputs[step_index].astype(jnp.float32) + attended.reshape(rows_dev, -1)).astype(
            jnp.bfloat16
        )
        chosen = expert_ids[step_index].reshape(-1)
        onehot = (chosen[:, None] == expert_range[None, :]).astype(jnp.int32)
        before = jnp.cumsum(onehot, axis=0) - onehot
        slot_rank = jnp.sum(before * onehot, axis=1)
        target = chosen * capacity + slot_rank
        placed = (target[:, None] == slot_columns[None, :]).reshape(rows_dev, TOPK, -1)
        spread = jnp.any(placed, axis=1).astype(jnp.bfloat16)
        outgoing = jnp.einsum(
            "rc,rd->cd", spread, hidden, preferred_element_type=jnp.float32
        ).astype(jnp.bfloat16)
        outgoing = outgoing.reshape(experts_all, capacity, -1)
        mixing = jnp.sum(jnp.where(placed, route_weights[step_index][:, :, None], 0.0), axis=1)
        arrived = lax.all_to_all(outgoing, "expert", split_axis=0, concat_axis=0, tiled=True)
        num_slots, item_count, feature_dim = arrived.shape
        tokens = arrived.reshape(num_slots * item_count, feature_dim)
        gate_val = jnp.dot(tokens, gate_mat, preferred_element_type=jnp.float32)
        up_val = jnp.dot(tokens, up_mat, preferred_element_type=jnp.float32)
        activated = (jax.nn.silu(gate_val) * up_val).astype(jnp.bfloat16)
        expert_out = jnp.dot(activated, down_mat, preferred_element_type=jnp.float32).astype(
            jnp.bfloat16
        )
        returned = lax.all_to_all(
            expert_out.reshape(num_slots, item_count, feature_dim),
            "expert",
            split_axis=0,
            concat_axis=0,
            tiled=True,
        )
        combined = jnp.dot(
            mixing,
            returned.reshape(experts_all * capacity, -1).astype(jnp.float32),
            precision=lax.Precision.HIGHEST,
        )
        results.append((hidden.astype(jnp.float32) + combined).astype(jnp.bfloat16))
    return jnp.stack(results)


def dense_shards(
    inputs,
    queries,
    new_keys,
    new_values,
    key_cache,
    value_cache,
    cache_lengths,
    expert_ids,
    route_weights,
    w_gate,
    w_up,
    w_down,
):
    groups = lax.axis_size("group")
    experts_all = lax.axis_size("expert")
    me = lax.axis_index("group")
    rows_dev = inputs.shape[1]
    width = inputs.shape[2]
    part = w_gate.shape[2] // groups
    depth = w_gate.shape[1]
    columns = w_down.shape[2]
    gate_full = jnp.zeros((width, part), w_gate.dtype)
    up_full = jnp.zeros((width, part), w_gate.dtype)
    down_full = jnp.zeros((part, width), w_gate.dtype)
    pairs = []
    for shift in range(groups):
        target = lax.rem(me + shift, groups)
        pieces = (
            lax.dynamic_slice_in_dim(w_gate[0], target * part, part, 1),
            lax.dynamic_slice_in_dim(w_up[0], target * part, part, 1),
            lax.dynamic_slice_in_dim(w_down[0], target * part, part, 0),
        )
        if shift:
            perm = [(i, (i + shift) % groups) for i in range(groups)]
            pieces = tuple(lax.ppermute(piece, "group", perm) for piece in pieces)
        pairs.append((lax.rem(me - shift + groups, groups), pieces))
    for source, (gate_piece, up_piece, down_piece) in pairs:
        gate_full = lax.dynamic_update_slice_in_dim(gate_full, gate_piece, source * depth, 0)
        up_full = lax.dynamic_update_slice_in_dim(up_full, up_piece, source * depth, 0)
        down_full = lax.dynamic_update_slice_in_dim(down_full, down_piece, source * columns, 1)
    hidden = attend_steps(
        inputs, queries, new_keys, new_values, key_cache, value_cache, cache_lengths
    )
    expert_range = jnp.arange(experts_all, dtype=jnp.int32)
    mixing = jnp.sum(
        jnp.where(
            expert_ids[..., None] == expert_range, route_weights[..., None], jnp.float32(0.0)
        ),
        axis=2,
    )
    mixing = mixing.reshape(STEPS * rows_dev, experts_all)
    flat = hidden.reshape(STEPS * rows_dev, width)
    tokens = gather_tree(flat).reshape(-1, width)
    factors = gather_tree(mixing).reshape(-1, experts_all)
    factor = lax.dynamic_slice_in_dim(factors, lax.axis_index("expert"), 1, 1)
    gate_val = jnp.dot(tokens, gate_full, preferred_element_type=jnp.float32)
    up_val = jnp.dot(tokens, up_full, preferred_element_type=jnp.float32)
    activated = (jax.nn.silu(gate_val) * up_val).astype(jnp.bfloat16)
    expert_out = jnp.dot(activated, down_full, preferred_element_type=jnp.float32)
    combined = scatter_tree(factor * expert_out, STEPS * rows_dev)
    out = flat.astype(jnp.float32) + combined
    return out.astype(jnp.bfloat16).reshape(STEPS, rows_dev, width)


def tree_stages():
    stages = [("group", lax.axis_size("group"), 1)]
    left = lax.axis_size("expert")
    inner = []
    stride = 1
    while left % 2 == 0 and len(inner) < 2:
        inner.append(("expert", 2, stride))
        stride, left = 2 * stride, left // 2
    if left > 1:
        inner.append(("expert", left, stride))
    return stages + inner[::-1]


def shift_stage(value, stage, shift):
    axis, size, stride = stage
    perm = []
    for i in range(lax.axis_size(axis)):
        digit = i // stride % size
        perm.append((i, i + ((digit + shift) % size - digit) * stride))
    return lax.ppermute(value, axis, perm)


def gather_tree(value):
    for stage in tree_stages():
        value = jnp.stack([value] + [shift_stage(value, stage, k) for k in range(1, stage[1])])
    return value


def scatter_tree(value, rows):
    for stage in tree_stages()[::-1]:
        value = value.reshape(stage[1], -1, value.shape[-1])
        total = value[0]
        for k in range(1, stage[1]):
            arrived = shift_stage(value[k].astype(jnp.bfloat16), stage, -k)
            total = total + arrived.astype(jnp.float32)
        value = total
    return value.reshape(rows, -1)


def attend_steps(inputs, queries, new_keys, new_values, key_cache, value_cache, cache_lengths):
    rows_dev = inputs.shape[1]
    per_group = HEADS // KV_HEADS
    key_rows = jnp.concatenate([key_cache, jnp.swapaxes(new_keys, 0, 1)], axis=1).reshape(
        rows_dev, CACHE + STEPS, KV_HEADS, HEAD_DIM
    )
    value_rows = jnp.concatenate([value_cache, jnp.swapaxes(new_values, 0, 1)], axis=1).reshape(
        rows_dev, CACHE + STEPS, KV_HEADS, HEAD_DIM
    )
    query_vals = queries.reshape(STEPS, rows_dev, KV_HEADS, per_group, HEAD_DIM)
    scores = jnp.einsum(
        "tbkgd,bjkd->bktgj", query_vals, key_rows, preferred_element_type=jnp.float32
    ) * (HEAD_DIM ** (-0.5))
    place = jnp.arange(CACHE + STEPS, dtype=jnp.int32)
    step = jnp.arange(STEPS, dtype=jnp.int32)
    ok_old = place[None, None, :] < cache_lengths[:, None, None]
    ok_new = (place[None, :] >= CACHE) & (place[None, :] - CACHE <= step[:, None])
    ok = ok_old & (place < CACHE) | ok_new[None]
    scores = jnp.where(ok[:, None, :, None, :], scores, -1e30)
    highest = jnp.max(scores, axis=-1, keepdims=True)
    weights = jnp.exp(scores - highest)
    probs = (weights / jnp.sum(weights, axis=-1, keepdims=True)).astype(jnp.bfloat16)
    attended = jnp.einsum(
        "bktgj,bjkd->tbkgd", probs, value_rows, preferred_element_type=jnp.float32
    )
    return (inputs.astype(jnp.float32) + attended.reshape(inputs.shape)).astype(jnp.bfloat16)


def pick_plan(*args):
    rows_dev = args[0].shape[1]
    capacity = max(2, 2 * rows_dev * TOPK // lax.axis_size("expert"))
    if capacity >= rows_dev:
        return dense_shards(*args)
    return shards(*args)


def solution(mesh):
    in_specs = (
        P(None, ("group", "expert"), None),
        P(None, ("group", "expert"), None),
        P(None, ("group", "expert"), None),
        P(None, ("group", "expert"), None),
        P(("group", "expert"), None, None),
        P(("group", "expert"), None, None),
        P(("group", "expert")),
        P(None, ("group", "expert"), None),
        P(None, ("group", "expert"), None),
        P("expert", "group", None),
        P("expert", "group", None),
        P("expert", None, "group"),
    )
    out_specs = P(None, ("group", "expert"), None)
    return jax.shard_map(pick_plan, mesh=mesh, in_specs=in_specs, out_specs=out_specs, check_vma=False)
```

```python
import jax
import jax.numpy as jnp
from jax import lax
from jax.sharding import PartitionSpec as P

HEADS = 32
KV_HEADS = 2
HEAD_DIM = 64
TOPK = 8
CACHE = 384
STEPS = 3


def attend_rows(query_vals, key_rows, value_rows, cache_ok, fresh_keys, fresh_values):
    factor = HEAD_DIM ** (-0.5)
    old_scores = (
        jnp.einsum("bkgd,bjkd->bkgj", query_vals, key_rows, preferred_element_type=jnp.float32)
        * factor
    )
    old_scores = jnp.where(cache_ok[:, None, None, :], old_scores, -1e30)
    new_scores = (
        jnp.einsum("bkgd,bjkd->bkgj", query_vals, fresh_keys, preferred_element_type=jnp.float32)
        * factor
    )
    highest = jnp.maximum(
        jnp.max(old_scores, axis=-1, keepdims=True), jnp.max(new_scores, axis=-1, keepdims=True)
    )
    old_weights = jnp.exp(old_scores - highest)
    new_weights = jnp.exp(new_scores - highest)
    denom_sum = jnp.sum(old_weights, axis=-1, keepdims=True) + jnp.sum(
        new_weights, axis=-1, keepdims=True
    )
    old_probs = (old_weights / denom_sum).astype(jnp.bfloat16)
    new_probs = (new_weights / denom_sum).astype(jnp.bfloat16)
    attended = jnp.einsum(
        "bkgj,bjkd->bkgd", old_probs, value_rows, preferred_element_type=jnp.float32
    )
    return attended + jnp.einsum(
        "bkgj,bjkd->bkgd", new_probs, fresh_values, preferred_element_type=jnp.float32
    )


def shards(
    inputs,
    queries,
    new_keys,
    new_values,
    key_cache,
    value_cache,
    cache_lengths,
    expert_ids,
    route_weights,
    w_gate,
    w_up,
    w_down,
):
    experts_all = lax.axis_size("expert")
    rows_dev = inputs.shape[1]
    per_group = HEADS // KV_HEADS
    capacity = max(2, 2 * rows_dev * TOPK // experts_all)
    gate_full, up_full, down_full = (
        lax.all_gather(w_gate, "group", axis=1, tiled=True),
        lax.all_gather(w_up, "group", axis=1, tiled=True),
        lax.all_gather(w_down, "group", axis=2, tiled=True),
    )
    gate_mat = gate_full[0]
    up_mat = up_full[0]
    down_mat = down_full[0]
    key_rows = key_cache.reshape(rows_dev, CACHE, KV_HEADS, HEAD_DIM)
    value_rows = value_cache.reshape(rows_dev, CACHE, KV_HEADS, HEAD_DIM)
    cache_ok = jnp.arange(CACHE, dtype=jnp.int32)[None, :] < cache_lengths[:, None]
    slot_columns = jnp.arange(experts_all * capacity, dtype=jnp.int32)
    expert_range = jnp.arange(experts_all, dtype=jnp.int32)
    results = []
    for step_index in range(STEPS):
        fresh = step_index + 1
        fresh_keys = jnp.swapaxes(new_keys[:fresh], 0, 1).reshape(
            rows_dev, fresh, KV_HEADS, HEAD_DIM
        )
        fresh_values = jnp.swapaxes(new_values[:fresh], 0, 1).reshape(
            rows_dev, fresh, KV_HEADS, HEAD_DIM
        )
        query_vals = queries[step_index].reshape(rows_dev, KV_HEADS, per_group, HEAD_DIM)
        attended = attend_rows(query_vals, key_rows, value_rows, cache_ok, fresh_keys, fresh_values)
        hidden = (inputs[step_index].astype(jnp.float32) + attended.reshape(rows_dev, -1)).astype(
            jnp.bfloat16
        )
        chosen = expert_ids[step_index].reshape(-1)
        onehot = (chosen[:, None] == expert_range[None, :]).astype(jnp.int32)
        before = jnp.cumsum(onehot, axis=0) - onehot
        slot_rank = jnp.sum(before * onehot, axis=1)
        target = chosen * capacity + slot_rank
        placed = (target[:, None] == slot_columns[None, :]).reshape(rows_dev, TOPK, -1)
        spread = jnp.any(placed, axis=1).astype(jnp.bfloat16)
        outgoing = jnp.einsum(
            "rc,rd->cd", spread, hidden, preferred_element_type=jnp.float32
        ).astype(jnp.bfloat16)
        outgoing = outgoing.reshape(experts_all, capacity, -1)
        mixing = jnp.sum(jnp.where(placed, route_weights[step_index][:, :, None], 0.0), axis=1)
        arrived = lax.all_to_all(outgoing, "expert", split_axis=0, concat_axis=0, tiled=True)
        num_slots, item_count, feature_dim = arrived.shape
        tokens = arrived.reshape(num_slots * item_count, feature_dim)
        gate_val = jnp.dot(tokens, gate_mat, preferred_element_type=jnp.float32)
        up_val = jnp.dot(tokens, up_mat, preferred_element_type=jnp.float32)
        activated = (jax.nn.silu(gate_val) * up_val).astype(jnp.bfloat16)
        expert_out = jnp.dot(activated, down_mat, preferred_element_type=jnp.float32).astype(
            jnp.bfloat16
        )
        returned = lax.all_to_all(
            expert_out.reshape(num_slots, item_count, feature_dim),
            "expert",
            split_axis=0,
            concat_axis=0,
            tiled=True,
        )
        combined = jnp.dot(
            mixing,
            returned.reshape(experts_all * capacity, -1).astype(jnp.float32),
            precision=lax.Precision.HIGHEST,
        )
        results.append((hidden.astype(jnp.float32) + combined).astype(jnp.bfloat16))
    return jnp.stack(results)


def dense_shards(
    inputs,
    queries,
    new_keys,
    new_values,
    key_cache,
    value_cache,
    cache_lengths,
    expert_ids,
    route_weights,
    w_gate,
    w_up,
    w_down,
):
    groups = lax.axis_size("group")
    experts_all = lax.axis_size("expert")
    me = lax.axis_index("group")
    rows_dev = inputs.shape[1]
    width = inputs.shape[2]
    part = w_gate.shape[2] // groups
    depth = w_gate.shape[1]
    columns = w_down.shape[2]
    pairs = []
    for shift in range(groups):
        target = lax.rem(me + shift, groups)
        pieces = (
            lax.dynamic_slice_in_dim(w_gate[0], target * part, part, 1),
            lax.dynamic_slice_in_dim(w_up[0], target * part, part, 1),
            lax.dynamic_slice_in_dim(w_down[0], target * part, part, 0),
        )
        if shift:
            perm = [(i, (i + shift) % groups) for i in range(groups)]
            pieces = tuple(lax.ppermute(piece, "group", perm) for piece in pieces)
        pairs.append((lax.rem(me - shift + groups, groups), pieces))
    hidden = attend_steps(
        inputs, queries, new_keys, new_values, key_cache, value_cache, cache_lengths
    )
    expert_range = jnp.arange(experts_all, dtype=jnp.int32)
    mixing = jnp.sum(
        jnp.where(
            expert_ids[..., None] == expert_range, route_weights[..., None], jnp.float32(0.0)
        ),
        axis=2,
    )
    mixing = mixing.reshape(STEPS * rows_dev, experts_all)
    flat = hidden.reshape(STEPS * rows_dev, width)
    factors = gather_tree(mixing).reshape(-1, experts_all)
    factor = lax.dynamic_slice_in_dim(factors, lax.axis_index("expert"), 1, 1)
    stages = tree_stages()
    arriving = [piece for k in range(1, groups) for piece in pairs[k][1]]
    tokens = flat
    for number, stage in enumerate(stages):
        if number >= 2 and number - 2 < len(arriving):
            tokens, arriving[number - 2] = lax.optimization_barrier((tokens, arriving[number - 2]))
        tokens = gather_stage(tokens, stage)
    tokens = tokens.reshape(-1, width)
    gate_val, up_val, downs = 0.0, 0.0, []
    for k in range(groups):
        source, pieces = pairs[k]
        if k:
            pieces = arriving[3 * (k - 1) : 3 * k]
        share = lax.dynamic_slice_in_dim(tokens, source * depth, depth, 1)
        gate_val = gate_val + jnp.dot(share, pieces[0], preferred_element_type=jnp.float32)
        up_val = up_val + jnp.dot(share, pieces[1], preferred_element_type=jnp.float32)
        downs.append(pieces[2])
    activated = (jax.nn.silu(gate_val) * up_val).astype(jnp.bfloat16)
    expert_out = jnp.dot(
        activated, jnp.concatenate(downs, axis=1), preferred_element_type=jnp.float32
    )
    combined = scatter_tree(factor * expert_out, stages[1:])
    combined = combined.reshape(-1, groups, columns)
    combined = jnp.concatenate(
        [
            lax.dynamic_index_in_dim(combined, lax.rem(me - at + groups, groups), 1, keepdims=False)
            for at in range(groups)
        ],
        axis=1,
    )
    combined = scatter_tree(combined, stages[:1]).reshape(STEPS * rows_dev, width)
    out = flat.astype(jnp.float32) + combined
    return out.astype(jnp.bfloat16).reshape(STEPS, rows_dev, width)


def tree_stages():
    stages = [("group", lax.axis_size("group"), 1)]
    left = lax.axis_size("expert")
    inner = []
    stride = 1
    while left % 2 == 0 and len(inner) < 2:
        inner.append(("expert", 2, stride))
        stride, left = 2 * stride, left // 2
    if left > 1:
        inner.append(("expert", left, stride))
    return stages + inner[::-1]


def shift_stage(value, stage, shift):
    axis, size, stride = stage
    perm = []
    for i in range(lax.axis_size(axis)):
        digit = i // stride % size
        perm.append((i, i + ((digit + shift) % size - digit) * stride))
    return lax.ppermute(value, axis, perm)


def gather_stage(value, stage):
    return jnp.stack([value] + [shift_stage(value, stage, k) for k in range(1, stage[1])])


def gather_tree(value):
    for stage in tree_stages():
        value = gather_stage(value, stage)
    return value


def scatter_tree(value, stages):
    for stage in stages[::-1]:
        value = value.reshape(stage[1], -1, value.shape[-1])
        total = value[0]
        for k in range(1, stage[1]):
            arrived = shift_stage(value[k].astype(jnp.bfloat16), stage, -k)
            total = total + arrived.astype(jnp.float32)
        value = total
    return value


def attend_steps(inputs, queries, new_keys, new_values, key_cache, value_cache, cache_lengths):
    rows_dev = inputs.shape[1]
    per_group = HEADS // KV_HEADS
    key_rows = jnp.concatenate([key_cache, jnp.swapaxes(new_keys, 0, 1)], axis=1).reshape(
        rows_dev, CACHE + STEPS, KV_HEADS, HEAD_DIM
    )
    value_rows = jnp.concatenate([value_cache, jnp.swapaxes(new_values, 0, 1)], axis=1).reshape(
        rows_dev, CACHE + STEPS, KV_HEADS, HEAD_DIM
    )
    query_vals = queries.reshape(STEPS, rows_dev, KV_HEADS, per_group, HEAD_DIM)
    scores = jnp.einsum(
        "tbkgd,bjkd->bktgj", query_vals, key_rows, preferred_element_type=jnp.float32
    ) * (HEAD_DIM ** (-0.5))
    place = jnp.arange(CACHE + STEPS, dtype=jnp.int32)
    step = jnp.arange(STEPS, dtype=jnp.int32)
    ok_old = place[None, None, :] < cache_lengths[:, None, None]
    ok_new = (place[None, :] >= CACHE) & (place[None, :] - CACHE <= step[:, None])
    ok = ok_old & (place < CACHE) | ok_new[None]
    scores = jnp.where(ok[:, None, :, None, :], scores, -1e30)
    highest = jnp.max(scores, axis=-1, keepdims=True)
    weights = jnp.exp(scores - highest)
    probs = (weights / jnp.sum(weights, axis=-1, keepdims=True)).astype(jnp.bfloat16)
    attended = jnp.einsum(
        "bktgj,bjkd->tbkgd", probs, value_rows, preferred_element_type=jnp.float32
    )
    return (inputs.astype(jnp.float32) + attended.reshape(inputs.shape)).astype(jnp.bfloat16)


def pick_plan(*args):
    rows_dev = args[0].shape[1]
    capacity = max(2, 2 * rows_dev * TOPK // lax.axis_size("expert"))
    if capacity >= rows_dev:
        return dense_shards(*args)
    return shards(*args)


def solution(mesh):
    in_specs = (
        P(None, ("group", "expert"), None),
        P(None, ("group", "expert"), None),
        P(None, ("group", "expert"), None),
        P(None, ("group", "expert"), None),
        P(("group", "expert"), None, None),
        P(("group", "expert"), None, None),
        P(("group", "expert")),
        P(None, ("group", "expert"), None),
        P(None, ("group", "expert"), None),
        P("expert", "group", None),
        P("expert", "group", None),
        P("expert", None, "group"),
    )
    out_specs = P(None, ("group", "expert"), None)
    return jax.shard_map(pick_plan, mesh=mesh, in_specs=in_specs, out_specs=out_specs, check_vma=False)
```

```python
import jax
import jax.numpy as jnp
from jax import lax
from jax.sharding import PartitionSpec as P

HEADS = 32
KV_HEADS = 2
HEAD_DIM = 64
TOPK = 8
CACHE = 384
STEPS = 3


def attend_rows(query_vals, key_rows, value_rows, cache_ok, fresh_keys, fresh_values):
    factor = HEAD_DIM ** (-0.5)
    old_scores = (
        jnp.einsum("bkgd,bjkd->bkgj", query_vals, key_rows, preferred_element_type=jnp.float32)
        * factor
    )
    old_scores = jnp.where(cache_ok[:, None, None, :], old_scores, -1e30)
    new_scores = (
        jnp.einsum("bkgd,bjkd->bkgj", query_vals, fresh_keys, preferred_element_type=jnp.float32)
        * factor
    )
    highest = jnp.maximum(
        jnp.max(old_scores, axis=-1, keepdims=True), jnp.max(new_scores, axis=-1, keepdims=True)
    )
    old_weights = jnp.exp(old_scores - highest)
    new_weights = jnp.exp(new_scores - highest)
    denom_sum = jnp.sum(old_weights, axis=-1, keepdims=True) + jnp.sum(
        new_weights, axis=-1, keepdims=True
    )
    old_probs = (old_weights / denom_sum).astype(jnp.bfloat16)
    new_probs = (new_weights / denom_sum).astype(jnp.bfloat16)
    attended = jnp.einsum(
        "bkgj,bjkd->bkgd", old_probs, value_rows, preferred_element_type=jnp.float32
    )
    return attended + jnp.einsum(
        "bkgj,bjkd->bkgd", new_probs, fresh_values, preferred_element_type=jnp.float32
    )


def shards(
    inputs,
    queries,
    new_keys,
    new_values,
    key_cache,
    value_cache,
    cache_lengths,
    expert_ids,
    route_weights,
    w_gate,
    w_up,
    w_down,
):
    experts_all = lax.axis_size("expert")
    rows_dev = inputs.shape[1]
    per_group = HEADS // KV_HEADS
    capacity = max(2, 2 * rows_dev * TOPK // experts_all)
    gate_full, up_full, down_full = (
        lax.all_gather(w_gate, "group", axis=1, tiled=True),
        lax.all_gather(w_up, "group", axis=1, tiled=True),
        lax.all_gather(w_down, "group", axis=2, tiled=True),
    )
    gate_mat = gate_full[0]
    up_mat = up_full[0]
    down_mat = down_full[0]
    key_rows = key_cache.reshape(rows_dev, CACHE, KV_HEADS, HEAD_DIM)
    value_rows = value_cache.reshape(rows_dev, CACHE, KV_HEADS, HEAD_DIM)
    cache_ok = jnp.arange(CACHE, dtype=jnp.int32)[None, :] < cache_lengths[:, None]
    slot_columns = jnp.arange(experts_all * capacity, dtype=jnp.int32)
    expert_range = jnp.arange(experts_all, dtype=jnp.int32)
    results = []
    for step_index in range(STEPS):
        fresh = step_index + 1
        fresh_keys = jnp.swapaxes(new_keys[:fresh], 0, 1).reshape(
            rows_dev, fresh, KV_HEADS, HEAD_DIM
        )
        fresh_values = jnp.swapaxes(new_values[:fresh], 0, 1).reshape(
            rows_dev, fresh, KV_HEADS, HEAD_DIM
        )
        query_vals = queries[step_index].reshape(rows_dev, KV_HEADS, per_group, HEAD_DIM)
        attended = attend_rows(query_vals, key_rows, value_rows, cache_ok, fresh_keys, fresh_values)
        hidden = (inputs[step_index].astype(jnp.float32) + attended.reshape(rows_dev, -1)).astype(
            jnp.bfloat16
        )
        chosen = expert_ids[step_index].reshape(-1)
        onehot = (chosen[:, None] == expert_range[None, :]).astype(jnp.int32)
        before = jnp.cumsum(onehot, axis=0) - onehot
        slot_rank = jnp.sum(before * onehot, axis=1)
        target = chosen * capacity + slot_rank
        placed = (target[:, None] == slot_columns[None, :]).reshape(rows_dev, TOPK, -1)
        spread = jnp.any(placed, axis=1).astype(jnp.bfloat16)
        outgoing = jnp.einsum(
            "rc,rd->cd", spread, hidden, preferred_element_type=jnp.float32
        ).astype(jnp.bfloat16)
        outgoing = outgoing.reshape(experts_all, capacity, -1)
        mixing = jnp.sum(jnp.where(placed, route_weights[step_index][:, :, None], 0.0), axis=1)
        arrived = lax.all_to_all(outgoing, "expert", split_axis=0, concat_axis=0, tiled=True)
        num_slots, item_count, feature_dim = arrived.shape
        tokens = arrived.reshape(num_slots * item_count, feature_dim)
        gate_val = jnp.dot(tokens, gate_mat, preferred_element_type=jnp.float32)
        up_val = jnp.dot(tokens, up_mat, preferred_element_type=jnp.float32)
        activated = (jax.nn.silu(gate_val) * up_val).astype(jnp.bfloat16)
        expert_out = jnp.dot(activated, down_mat, preferred_element_type=jnp.float32).astype(
            jnp.bfloat16
        )
        returned = lax.all_to_all(
            expert_out.reshape(num_slots, item_count, feature_dim),
            "expert",
            split_axis=0,
            concat_axis=0,
            tiled=True,
        )
        combined = jnp.dot(
            mixing,
            returned.reshape(experts_all * capacity, -1).astype(jnp.float32),
            precision=lax.Precision.HIGHEST,
        )
        results.append((hidden.astype(jnp.float32) + combined).astype(jnp.bfloat16))
    return jnp.stack(results)


def dense_shards(
    inputs,
    queries,
    new_keys,
    new_values,
    key_cache,
    value_cache,
    cache_lengths,
    expert_ids,
    route_weights,
    w_gate,
    w_up,
    w_down,
):
    groups = lax.axis_size("group")
    experts_all = lax.axis_size("expert")
    me = lax.axis_index("group")
    rows_dev = inputs.shape[1]
    width = inputs.shape[2]
    part = w_gate.shape[2] // groups
    depth = w_gate.shape[1]
    columns = w_down.shape[2]
    pairs = []
    for shift in range(groups):
        target = lax.rem(me + shift, groups)
        pieces = (
            lax.dynamic_slice_in_dim(w_gate[0], target * part, part, 1),
            lax.dynamic_slice_in_dim(w_up[0], target * part, part, 1),
            lax.dynamic_slice_in_dim(w_down[0], target * part, part, 0),
        )
        if shift:
            perm = [(i, (i + shift) % groups) for i in range(groups)]
            pieces = tuple(lax.ppermute(piece, "group", perm) for piece in pieces)
        pairs.append((lax.rem(me - shift + groups, groups), pieces))
    hidden = attend_steps(
        inputs, queries, new_keys, new_values, key_cache, value_cache, cache_lengths
    )
    expert_range = jnp.arange(experts_all, dtype=jnp.int32)
    mixing = jnp.sum(
        jnp.where(
            expert_ids[..., None] == expert_range, route_weights[..., None], jnp.float32(0.0)
        ),
        axis=2,
    )
    mixing = mixing.reshape(STEPS * rows_dev, experts_all)
    flat = hidden.reshape(STEPS * rows_dev, width)
    factors = gather_tree(mixing).reshape(-1, experts_all)
    factor = lax.dynamic_slice_in_dim(factors, lax.axis_index("expert"), 1, 1)
    stages = tree_stages()
    arriving = [piece for k in range(1, groups) for piece in pairs[k][1]]
    tokens = flat
    for number, stage in enumerate(stages):
        if number == 2:
            tokens, arriving[:2] = lax.optimization_barrier((tokens, arriving[:2]))
        elif number == 3:
            tokens, arriving[2:] = lax.optimization_barrier((tokens, arriving[2:]))
        tokens = gather_stage(tokens, stage)
    tokens = tokens.reshape(-1, width)
    gate_val, up_val, downs = 0.0, 0.0, []
    for k in range(groups):
        source, pieces = pairs[k]
        if k:
            pieces = arriving[3 * (k - 1) : 3 * k]
        share = lax.dynamic_slice_in_dim(tokens, source * depth, depth, 1)
        gate_val = gate_val + jnp.dot(share, pieces[0], preferred_element_type=jnp.float32)
        up_val = up_val + jnp.dot(share, pieces[1], preferred_element_type=jnp.float32)
        downs.append(pieces[2])
    activated = (jax.nn.silu(gate_val) * up_val).astype(jnp.bfloat16)
    expert_out = jnp.dot(
        activated, jnp.concatenate(downs, axis=1), preferred_element_type=jnp.float32
    )
    combined = scatter_tree(factor * expert_out, stages[1:])
    combined = combined.reshape(-1, groups, columns)
    combined = jnp.concatenate(
        [
            lax.dynamic_index_in_dim(combined, lax.rem(me - at + groups, groups), 1, keepdims=False)
            for at in range(groups)
        ],
        axis=1,
    )
    combined = scatter_tree(combined, stages[:1]).reshape(STEPS * rows_dev, width)
    out = flat.astype(jnp.float32) + combined
    return out.astype(jnp.bfloat16).reshape(STEPS, rows_dev, width)


def tree_stages():
    stages = [("group", lax.axis_size("group"), 1)]
    left = lax.axis_size("expert")
    inner = []
    stride = 1
    while left % 2 == 0 and len(inner) < 2:
        inner.append(("expert", 2, stride))
        stride, left = 2 * stride, left // 2
    if left > 1:
        inner.append(("expert", left, stride))
    return stages + inner[::-1]


def shift_stage(value, stage, shift):
    axis, size, stride = stage
    perm = []
    for i in range(lax.axis_size(axis)):
        digit = i // stride % size
        perm.append((i, i + ((digit + shift) % size - digit) * stride))
    return lax.ppermute(value, axis, perm)


def gather_stage(value, stage):
    return jnp.stack([value] + [shift_stage(value, stage, k) for k in range(1, stage[1])])


def gather_tree(value):
    for stage in tree_stages():
        value = gather_stage(value, stage)
    return value


def scatter_tree(value, stages):
    for stage in stages[::-1]:
        value = value.reshape(stage[1], -1, value.shape[-1])
        total = value[0]
        for k in range(1, stage[1]):
            arrived = shift_stage(value[k].astype(jnp.bfloat16), stage, -k)
            total = total + arrived.astype(jnp.float32)
        value = total
    return value


def attend_steps(inputs, queries, new_keys, new_values, key_cache, value_cache, cache_lengths):
    rows_dev = inputs.shape[1]
    per_group = HEADS // KV_HEADS
    key_rows = jnp.concatenate([key_cache, jnp.swapaxes(new_keys, 0, 1)], axis=1).reshape(
        rows_dev, CACHE + STEPS, KV_HEADS, HEAD_DIM
    )
    value_rows = jnp.concatenate([value_cache, jnp.swapaxes(new_values, 0, 1)], axis=1).reshape(
        rows_dev, CACHE + STEPS, KV_HEADS, HEAD_DIM
    )
    query_vals = queries.reshape(STEPS, rows_dev, KV_HEADS, per_group, HEAD_DIM)
    scores = jnp.einsum(
        "tbkgd,bjkd->bktgj", query_vals, key_rows, preferred_element_type=jnp.float32
    ) * (HEAD_DIM ** (-0.5))
    place = jnp.arange(CACHE + STEPS, dtype=jnp.int32)
    step = jnp.arange(STEPS, dtype=jnp.int32)
    ok_old = place[None, None, :] < cache_lengths[:, None, None]
    ok_new = (place[None, :] >= CACHE) & (place[None, :] - CACHE <= step[:, None])
    ok = ok_old & (place < CACHE) | ok_new[None]
    scores = jnp.where(ok[:, None, :, None, :], scores, -1e30)
    highest = jnp.max(scores, axis=-1, keepdims=True)
    weights = jnp.exp(scores - highest)
    probs = (weights / jnp.sum(weights, axis=-1, keepdims=True)).astype(jnp.bfloat16)
    attended = jnp.einsum(
        "bktgj,bjkd->tbkgd", probs, value_rows, preferred_element_type=jnp.float32
    )
    return (inputs.astype(jnp.float32) + attended.reshape(inputs.shape)).astype(jnp.bfloat16)


def pick_plan(*args):
    rows_dev = args[0].shape[1]
    capacity = max(2, 2 * rows_dev * TOPK // lax.axis_size("expert"))
    if capacity >= rows_dev:
        return dense_shards(*args)
    return shards(*args)


def solution(mesh):
    in_specs = (
        P(None, ("group", "expert"), None),
        P(None, ("group", "expert"), None),
        P(None, ("group", "expert"), None),
        P(None, ("group", "expert"), None),
        P(("group", "expert"), None, None),
        P(("group", "expert"), None, None),
        P(("group", "expert")),
        P(None, ("group", "expert"), None),
        P(None, ("group", "expert"), None),
        P("expert", "group", None),
        P("expert", "group", None),
        P("expert", None, "group"),
    )
    out_specs = P(None, ("group", "expert"), None)
    return jax.shard_map(pick_plan, mesh=mesh, in_specs=in_specs, out_specs=out_specs, check_vma=False)
```
